32 devices in a mesh: dom: 8 (over y, x, core), tm: 4 (over z).
Axes of the slice: x: 2, y: 2, z: 4, core: 2. Of those that a mesh axis runs over, the one named last changes fastest.
Arguments:
- features: bfloat16 [4, 2048, 512], P('tm', 'dom'), may hold values from -6 to 6
- tile_rows: int32 [4, 192], P('tm', 'dom'), may hold values from 0 to 15, as said below
- tile_cols: int32 [4, 192], P('tm', 'dom'), may hold values from 0 to 15, as said below
- tile_vals: bfloat16 [4, 192, 128, 128], P('tm', 'dom'), may hold values from 0 to 0.0625
- tile_used: int32 [4, 8], P('tm', 'dom'), may hold values from 12 to 24, as said below
- pool_weight: bfloat16 [512, 512], replicated, may hold values from -0.25 to 0.25
- w_in: bfloat16 [3, 512, 512], replicated, may hold values from -0.25 to 0.25
- w_state: bfloat16 [3, 512, 512], replicated, may hold values from -0.25 to 0.25
- gate_offset: float32 [512], replicated, may hold values from 0 to 5
- start_weight: float32 [512, 512], replicated, may hold values from -3 to 3
Outputs:
- hidden_out: bfloat16 [4, 2048, 512], P('tm', 'dom')
- weights_out: float32 [4, 512, 512], P('tm')
The draws below stay inside these ranges and needn't reach their ends.
Inputs may be any that keep to these rules, and one draw needn't show every extreme that they name: `tile_rows`: every slot of row partition d names a row block of that partition, d * 2 to (d + 1) * 2 - 1. `tile_cols`: within one snapshot and one row partition, all slots whose column blocks lie on the same dom index name the same column block. `tile_used`: in every snapshot some row partition has all 24 slots live.
All inputs are finite; a program needn't handle non-finite values.
Results may differ from the reference program's by a relative error of at most 0.017.
Values may be sent and summed in bfloat16 or wider, within the bound.
A program may use at most 64 MiB of HBM per device.

```python
import jax
import jax.numpy as jnp
from jax import lax

D = 512
BLOCK = 128
TILES_DEV = 24
RB_DEV = 2
NODES = 2048
SNAPS = 4
SLOTS = 192
N_DOM = 8


def draw_tile_rows(key, part):
    offsets = jax.random.randint(key, (SNAPS, N_DOM, TILES_DEV), 0, RB_DEV)
    row_base = (jnp.arange(N_DOM, dtype=jnp.int32) * RB_DEV)[None, :, None]
    return (offsets + row_base).reshape(SNAPS, N_DOM * TILES_DEV).astype(jnp.int32)


def draw_tile_cols(key, part):
    pick_key, peer_key = jax.random.split(key)
    block_picks = jax.random.randint(pick_key, (SNAPS, N_DOM, N_DOM), 0, RB_DEV)
    peer_draw = jax.random.randint(peer_key, (SNAPS, N_DOM, TILES_DEV), 0, N_DOM)
    chosen = jnp.take_along_axis(block_picks, peer_draw, axis=2)
    return (peer_draw * RB_DEV + chosen).reshape(SNAPS, N_DOM * TILES_DEV).astype(jnp.int32)


def draw_tile_used(key, part):
    count_key, full_key = jax.random.split(key)
    counts = jax.random.randint(count_key, (SNAPS, N_DOM), TILES_DEV // 2, TILES_DEV + 1)
    full_at = jax.random.randint(full_key, (SNAPS,), 0, N_DOM)
    positions = jnp.arange(N_DOM, dtype=jnp.int32)[None, :]
    return jnp.where(positions == full_at[:, None], TILES_DEV, counts).astype(jnp.int32)


def steps_of(own_key, extent, pieces, smallest, largest):
    gain = 1.0
    for dim, shards_of in pieces:
        steps = jax.random.uniform(jax.random.fold_in(jax.random.fold_in(own_key, 6), dim), (shards_of,), jnp.float32, smallest / len(pieces), largest / len(pieces))
        gain = gain * jnp.repeat(jnp.exp(steps), extent[dim] // shards_of).reshape((-1,) + (1,) * (len(extent) - 1 - dim))
    return gain


def scatter_about(rng, dims, spread, bound, cuts=(), kind=jnp.bfloat16):
    values = jax.random.normal(rng, dims, jnp.float32) * spread
    if len(cuts) > 0:
        values = steps_of(rng, dims, cuts, -0.22, 0.18) * values
    return jnp.clip(values, min=-bound, max=bound).astype(kind)


def setup_inputs(seed: int = 0) -> dict:
    splits = jax.random.split(jax.random.key(seed), 11)
    return {
        "features": scatter_about(splits[0], (SNAPS, NODES, D), 1.0, 6.0, ((0, 4), (1, 8))),
        "tile_rows": draw_tile_rows(jax.random.fold_in(splits[10], 71), 0),
        "tile_cols": draw_tile_cols(jax.random.fold_in(splits[10], 71), 0),
        "tile_vals": jnp.clip(0.0625 * jax.random.uniform(splits[3], (SNAPS, SLOTS, BLOCK, BLOCK), jnp.float32) ** steps_of(splits[3], (SNAPS, SLOTS, BLOCK, BLOCK), ((0, 4), (1, 8)), -0.2, 0.2), 0.0, 0.0625).astype(jnp.bfloat16),
        "tile_used": draw_tile_used(jax.random.fold_in(splits[10], 71), 0),
        "pool_weight": scatter_about(splits[5], (D, D), D ** -0.5, 0.25),
        "w_in": scatter_about(splits[6], (3, D, D), D ** -0.5, 0.25),
        "w_state": scatter_about(splits[7], (3, D, D), D ** -0.5, 0.25),
        "gate_offset": jnp.clip(jax.random.uniform(splits[8], (D,), jnp.float32, 0.0, 5.0), 0.0, 5.0),
        "start_weight": scatter_about(splits[9], (D, D), 0.5, 3.0, (), jnp.float32),
    }


def gru_step(state, inputs_t, w_state, gate_offset):
    state_b = state.astype(jnp.bfloat16)
    upd_pre = jnp.dot(w_state[0], state_b, preferred_element_type=jnp.float32)
    rst_pre = jnp.dot(w_state[1], state_b, preferred_element_type=jnp.float32)
    update = jax.nn.sigmoid(inputs_t[0] + upd_pre - gate_offset[:, None])
    reset = jax.nn.sigmoid(inputs_t[1] + rst_pre)
    reset_state = (reset * state).astype(jnp.bfloat16)
    candidate = jnp.tanh(inputs_t[2] + jnp.dot(w_state[2], reset_state, preferred_element_type=jnp.float32))
    return (1.0 - update) * state + update * candidate


def reference(features, tile_rows, tile_cols, tile_vals, tile_used, pool_weight, w_in, w_state, gate_offset, start_weight):
    num_blocks = NODES // BLOCK

    def aggregate(inputs):
        snap_feats, rows_blk, cols_blk, tile_block, live_count = inputs
        blocks = snap_feats.reshape(num_blocks, BLOCK, D)
        source = jnp.take(blocks, cols_blk.astype(jnp.int32), axis=0).astype(jnp.float32)
        product = jnp.einsum("jab,jbd->jad", tile_block.astype(jnp.float32), source)
        slot_ids = jnp.arange(N_DOM * TILES_DEV, dtype=jnp.int32)
        valid_mask = (slot_ids % TILES_DEV) < live_count[slot_ids // TILES_DEV]
        product = product * valid_mask.astype(jnp.float32)[:, None, None]
        summed = jax.ops.segment_sum(product, rows_blk.astype(jnp.int32), num_segments=num_blocks)
        return (snap_feats.astype(jnp.float32) + summed.reshape(NODES, D)).astype(jnp.bfloat16)

    aggregated = lax.map(aggregate, (features, tile_rows, tile_cols, tile_vals, tile_used))

    def summarize(snap_feats):
        pool_gates = jax.nn.sigmoid(jnp.dot(snap_feats, pool_weight, preferred_element_type=jnp.float32)).astype(jnp.bfloat16)
        pooled = jnp.dot(snap_feats.T, pool_gates, preferred_element_type=jnp.float32)
        return (pooled * NODES ** -0.5).astype(jnp.bfloat16)

    summary = lax.map(summarize, features)
    in_side = jnp.einsum("gij,tjk->tgik", w_in.astype(jnp.float32), summary.astype(jnp.float32))

    def chain(state, inputs_t):
        new_state = gru_step(state, inputs_t, w_state, gate_offset)
        return new_state, new_state

    final_state, weights_out = lax.scan(chain, start_weight, in_side)

    def project(inputs):
        agg_rows, weight_t = inputs
        mixed = jnp.dot(agg_rows, weight_t.astype(jnp.bfloat16), preferred_element_type=jnp.float32)
        return jnp.maximum(mixed * D ** -0.5, 0.0).astype(jnp.bfloat16)

    hidden_out = lax.map(project, (aggregated, weights_out))
    return hidden_out, weights_out
```

```python
import functools

import jax
import jax.numpy as jnp
from jax import lax
from jax.experimental import pallas as pl
from jax.experimental.pallas import tpu as pltpu
from jax.sharding import PartitionSpec as P

BLOCK = 128
LANES = 128
CORES = 2


def xor(q, k, bits):
    out = 0
    for b in range(bits):
        out = out + (((q // (1 << b)) + ((k >> b) & 1)) % 2) * (1 << b)
    return out


def nt_dot(a, b):
    return lax.dot_general(a, b, (((1,), (1,)), ((), ())), preferred_element_type=jnp.float32)


def tn_dot(a, b):
    return lax.dot_general(a, b, (((0,), (0,)), ((), ())), preferred_element_type=jnp.float32)


def kernel(
    n_dom,
    n_tm,
    feats_ref,
    rows_ref,
    cols_ref,
    vals_ref,
    used_ref,
    pool_ref,
    win_ref,
    wst_ref,
    off_ref,
    start_ref,
    hid_ref,
    wout_ref,
    feats,
    vals,
    pool,
    win,
    wst,
    off,
    state,
    sums,
    wfull,
    agg,
    load_sem,
    f_send,
    f_recv,
    ff_send,
    ff_recv,
    z_send,
    z_recv,
    zf_send,
    zf_recv,
    w_send,
    w_recv,
    wf_send,
    wf_recv,
):
    n_chips = n_dom // CORES
    bits = n_chips.bit_length() - 1
    blocks, _, width = feats_ref.shape
    slots = vals_ref.shape[0]
    groups = wfull.shape[0]
    half_k = LANES // CORES
    half_r = width // CORES
    rows_dev = blocks * BLOCK
    me = lax.axis_index("dom")
    t_me = lax.axis_index("tm")
    chip, core = me // CORES, me % CORES
    group = chip % groups
    partner = {"dom": chip * CORES + 1 - core}
    lane0 = pl.multiple_of(group * LANES, LANES)

    def same_core(k):
        return {"dom": xor(chip, k, bits) * CORES + core}

    def remote(src, dst, send, recv, to):
        return pltpu.make_async_remote_copy(
            src_ref=src, dst_ref=dst, send_sem=send, recv_sem=recv,
            device_id=to, device_id_type=pl.DeviceIdType.MESH,
        )

    def load(src, dst, i):
        copy = pltpu.make_async_copy(src, dst, load_sem.at[i])
        copy.start()
        return copy

    def piece(dev):
        return feats.at[pl.ds(dev * blocks, blocks)]

    loads = [
        load(feats_ref, piece(me), 0),
        load(pool_ref.at[:, pl.ds(lane0, LANES)], pool, 1),
        load(vals_ref, vals, 2),
        load(win_ref, win, 3),
        load(wst_ref, wst, 4),
        load(start_ref.at[:, pl.ds(lane0, LANES)], state, 5),
        load(off_ref, off, 6),
    ]

    barrier = pltpu.get_barrier_semaphore()
    greet = [partner] + [same_core(k) for k in range(1, n_chips)]
    greet += [{"tm": (t_me + o) % n_tm} for o in range(1, n_tm)]
    for to in greet:
        pl.semaphore_signal(barrier, inc=1, device_id=to, device_id_type=pl.DeviceIdType.MESH)
    pl.semaphore_wait(barrier, len(greet))

    f_out = [None] + [
        remote(feats_ref, piece(me), f_send.at[k], f_recv.at[k], same_core(k))
        for k in range(1, n_chips)
    ]
    for k in range(1, n_chips):
        f_out[k].start()
    ff_out = [remote(feats_ref, piece(me), ff_send.at[0], ff_recv.at[0], partner)]
    ff_out[0].start()

    loads[0].wait()
    loads[1].wait()

    def pooled(dev):
        f = feats[pl.ds(dev * blocks, blocks)].reshape(rows_dev, width)
        gates = jax.nn.sigmoid(jnp.dot(f, pool[...], preferred_element_type=jnp.float32))
        return tn_dot(gates.astype(jnp.bfloat16), f)

    total = pooled(me)
    ff_out[0].wait_recv()
    total = total + pooled(chip * CORES + 1 - core)
    for k in range(1, n_chips):
        dev = xor(chip, k, bits) * CORES
        f_out[k].wait_recv()
        ff_out.append(
            remote(piece(dev + core), piece(dev + core), ff_send.at[k], ff_recv.at[k], partner)
        )
        ff_out[k].start()
        total = total + pooled(dev + core)
    for k in range(1, n_chips):
        dev = xor(chip, k, bits) * CORES
        ff_out[k].wait_recv()
        total = total + pooled(dev + 1 - core)
    sums[t_me] = (total * (rows_dev * n_dom) ** (-0.5)).astype(jnp.bfloat16)

    my_half = pl.ds(core * half_k, half_k)
    z_out = []
    for o in range(1, n_tm):
        z_out.append(
            remote(
                sums.at[t_me, my_half], sums.at[t_me, my_half],
                z_send.at[o], z_recv.at[t_me], {"tm": (t_me + o) % n_tm},
            )
        )
        z_out[-1].start()

    loads[2].wait()
    masked = []
    sources = []
    for j in range(slots):
        tile = vals[j]
        live = j < used_ref[0, 0]
        row = rows_ref[0, j] - me * blocks
        masked.append(
            jnp.concatenate(
                [jnp.where(live & (row == b), tile, jnp.zeros_like(tile)) for b in range(blocks)],
                axis=0,
            )
        )
        sources.append(feats[cols_ref[0, j]])
    own = feats[pl.ds(me * blocks, blocks)].reshape(rows_dev, width).astype(jnp.float32)
    summed = jnp.dot(
        jnp.concatenate(masked, axis=1),
        jnp.concatenate(sources, axis=0),
        preferred_element_type=jnp.float32,
    )
    agg[...] = (own + summed).astype(jnp.bfloat16)

    def z_forward(t):
        ref = sums.at[t, my_half]
        return remote(ref, ref, zf_send.at[t], zf_recv.at[t], partner)

    for t in range(n_tm):
        @pl.when(t_me != t)
        def _(t=t):
            ref = sums.at[t, my_half]
            remote(ref, ref, z_send.at[0], z_recv.at[t], partner).wait_recv()
            z_forward(t).start()

    for i in range(3, 7):
        loads[i].wait()
    offset = jnp.transpose(jnp.broadcast_to(off[...], (LANES, width)))
    for t in range(n_tm):
        @pl.when(t_me != t)
        def _(t=t):
            z_forward(t).wait_recv()

        summary = sums[t]
        now = state[...]
        now_b = now.astype(jnp.bfloat16)
        reset = jax.nn.sigmoid(
            nt_dot(win[1], summary) + jnp.dot(wst[1], now_b, preferred_element_type=jnp.float32)
        )
        reset_state = (reset * now).astype(jnp.bfloat16)
        update = jax.nn.sigmoid(
            nt_dot(win[0], summary)
            + jnp.dot(wst[0], now_b, preferred_element_type=jnp.float32)
            - offset
        )
        candidate = jnp.tanh(
            nt_dot(win[2], summary)
            + jnp.dot(wst[2], reset_state, preferred_element_type=jnp.float32)
        )
        new = (1.0 - update) * now + update * candidate
        state[...] = new

        @pl.when(t_me == t)
        def _(new=new):
            wfull[group] = new.astype(jnp.bfloat16)

    w_half = pl.ds(core * half_r, half_r)
    w_out = [None]
    for k in range(1, groups):
        ref = wfull.at[group, w_half]
        w_out.append(remote(ref, ref, w_send.at[k], w_recv.at[k], same_core(k)))
        w_out[k].start()

    def emit(g):
        w = wfull[g]
        lanes = pl.ds(pl.multiple_of(g * LANES, LANES), LANES)
        mixed = jnp.dot(agg[...], w, preferred_element_type=jnp.float32)
        hid_ref[:, lanes] = jnp.maximum(mixed * width ** (-0.5), 0.0).astype(jnp.bfloat16)
        wout_ref[:, lanes] = w.astype(jnp.float32)

    emit(group)
    wf_out = [None]
    for k in range(1, groups):
        w_out[k].wait_recv()
        ref = wfull.at[xor(group, k, bits), w_half]
        wf_out.append(remote(ref, ref, wf_send.at[k], wf_recv.at[k], partner))
        wf_out[k].start()
    for k in range(1, groups):
        wf_out[k].wait_recv()
        emit(xor(group, k, bits))

    for k in range(1, n_chips):
        f_out[k].wait_send()
    for k in range(n_chips):
        ff_out[k].wait_send()
    for copy in z_out:
        copy.wait_send()
    for t in range(n_tm):
        @pl.when(t_me != t)
        def _(t=t):
            z_forward(t).wait_send()
    for k in range(1, groups):
        w_out[k].wait_send()
        wf_out[k].wait_send()


def shards(
    n_dom,
    n_tm,
    features,
    tile_rows,
    tile_cols,
    tile_vals,
    tile_used,
    pool_weight,
    w_in,
    w_state,
    gate_offset,
    start_weight,
):
    _, rows_dev, width = features.shape
    slots = tile_rows.shape[1]
    blocks = rows_dev // BLOCK
    n_chips = n_dom // CORES
    groups = width // LANES
    hbm = pl.BlockSpec(memory_space=pl.ANY)
    smem = pl.BlockSpec(memory_space=pltpu.SMEM)
    vmem = pl.BlockSpec(memory_space=pltpu.VMEM)
    dma = pltpu.SemaphoreType.DMA
    bf16 = jnp.bfloat16
    hidden, weights = pl.pallas_call(
        functools.partial(kernel, n_dom, n_tm),
        out_shape=(
            jax.ShapeDtypeStruct((rows_dev, width), bf16),
            jax.ShapeDtypeStruct((width, width), jnp.float32),
        ),
        in_specs=[hbm, smem, smem, hbm, smem, hbm, hbm, hbm, hbm, hbm],
        out_specs=(vmem, vmem),
        scratch_shapes=[
            pltpu.VMEM((n_dom * blocks, BLOCK, width), bf16),
            pltpu.VMEM((slots, BLOCK, BLOCK), bf16),
            pltpu.VMEM((width, LANES), bf16),
            pltpu.VMEM((3, width, width), bf16),
            pltpu.VMEM((3, width, width), bf16),
            pltpu.VMEM((1, width), jnp.float32),
            pltpu.VMEM((width, LANES), jnp.float32),
            pltpu.VMEM((n_tm, LANES, width), bf16),
            pltpu.VMEM((groups, width, LANES), bf16),
            pltpu.VMEM((rows_dev, width), bf16),
            dma((7,)),
            dma((n_chips,)),
            dma((n_chips,)),
            dma((n_chips,)),
            dma((n_chips,)),
            dma((n_tm,)),
            dma((n_tm,)),
            dma((n_tm,)),
            dma((n_tm,)),
            dma((groups,)),
            dma((groups,)),
            dma((groups,)),
            dma((groups,)),
        ],
        compiler_params=pltpu.CompilerParams(
            collective_id=0, has_side_effects=True, vmem_limit_bytes=48 * 1024 * 1024
        ),
    )(
        features.reshape(blocks, BLOCK, width),
        tile_rows,
        tile_cols,
        tile_vals.reshape(slots, BLOCK, BLOCK),
        tile_used,
        pool_weight,
        w_in,
        w_state,
        gate_offset.reshape(1, width),
        start_weight,
    )
    return hidden[None], weights[None]


def solution(mesh):
    in_specs = (
        P("tm", "dom", None),
        P("tm", "dom"),
        P("tm", "dom"),
        P("tm", "dom", None, None),
        P("tm", "dom"),
        P(),
        P(),
        P(),
        P(),
        P(),
    )
    out_specs = (P("tm", "dom", None), P("tm", None, None))
    body = functools.partial(shards, mesh.shape["dom"], mesh.shape["tm"])
    return jax.shard_map(body, mesh=mesh, in_specs=in_specs, out_specs=out_specs, check_vma=False)
```

```python
import functools

import jax
import jax.numpy as jnp
from jax import lax
from jax.experimental import pallas as pl
from jax.experimental.pallas import tpu as pltpu
from jax.sharding import PartitionSpec as P

BLOCK = 128
LANES = 128
CORES = 2


def xor(q, k, bits):
    out = 0
    for b in range(bits):
        out = out + (((q // (1 << b)) + ((k >> b) & 1)) % 2) * (1 << b)
    return out


def nt_dot(a, b):
    return lax.dot_general(a, b, (((1,), (1,)), ((), ())), preferred_element_type=jnp.float32)


def tn_dot(a, b):
    return lax.dot_general(a, b, (((0,), (0,)), ((), ())), preferred_element_type=jnp.float32)


def kernel(
    n_dom,
    n_tm,
    feats_ref,
    rows_in,
    cols_in,
    vals_ref,
    used_in,
    pool_ref,
    win_ref,
    wst_ref,
    off_ref,
    start_ref,
    hid_ref,
    wout_ref,
    feats,
    vals,
    pool,
    win,
    wst,
    off,
    start,
    part,
    part_b,
    pair_in,
    reduced,
    terms,
    sums,
    wfull,
    agg,
    mask,
    rows_ref,
    cols_ref,
    used_ref,
    load_sem,
    pair_sem,
    r_send,
    r_recv,
    f_send,
    f_recv,
    ff_send,
    ff_recv,
    z_send,
    z_recv,
    w_send,
    w_recv,
    wf_send,
    wf_recv,
):
    n_chips = n_dom // CORES
    bits = n_chips.bit_length() - 1
    blocks, _, width = feats_ref.shape
    slots = vals_ref.shape[0]
    groups = wfull.shape[0]
    half = LANES // CORES
    rows_dev = blocks * BLOCK
    me = lax.axis_index("dom")
    t_me = lax.axis_index("tm")
    chip, core = me // CORES, me % CORES
    group = chip % groups
    partner = {"dom": chip * CORES + 1 - core}
    lane0 = pl.multiple_of(group * LANES, LANES)

    def same_core(k):
        return {"dom": xor(chip, k, bits) * CORES + core}

    def remote(src, dst, send, recv, to):
        return pltpu.make_async_remote_copy(
            src_ref=src, dst_ref=dst, send_sem=send, recv_sem=recv,
            device_id=to, device_id_type=pl.DeviceIdType.MESH,
        )

    def load(src, dst, i):
        copy = pltpu.make_async_copy(src, dst, load_sem.at[i])
        copy.start()
        return copy

    def piece(dev):
        return feats.at[pl.ds(dev * blocks, blocks)]

    loads = [
        load(feats_ref, piece(me), 0),
        load(pool_ref, pool, 1),
        load(start_ref.at[:, pl.ds(lane0, LANES)], start, 2),
        load(win_ref, win, 3),
        load(wst_ref, wst, 4),
        load(off_ref, off, 5),
        load(vals_ref, vals, 6),
        load(rows_in, rows_ref, 7),
        load(cols_in, cols_ref, 8),
        load(used_in, used_ref, 9),
    ]

    barrier = pltpu.get_barrier_semaphore()
    greet = [partner] + [same_core(k) for k in range(1, n_chips)]
    greet += [{"tm": (t_me + o) % n_tm} for o in range(1, n_tm)]
    for to in greet:
        pl.semaphore_signal(barrier, inc=1, device_id=to, device_id_type=pl.DeviceIdType.MESH)

    orders = [list(range(bits)) if b % 2 == 0 else list(range(bits))[::-1] for b in range(blocks)]
    f_out, ff_out = {}, {}

    def forward(b, m):
        src = feats_ref.at[b] if m == 0 else slot(b, m)
        ff_out[b, m] = remote(src, slot(b, m), ff_send.at[b, m], ff_recv.at[b, m], partner)
        ff_out[b, m].start()

    def slot(b, m):
        return feats.at[(xor(chip, m, bits) * CORES + core) * blocks + b]

    def arrive(b, m):
        f_out[b, m].wait_recv()
        forward(b, m)

    def gather_stage(i):
        for b in range(blocks):
            held = [0]
            for d in orders[b][:i]:
                held = held + [m + (1 << d) for m in held]
            step = 1 << orders[b][i]
            for m in held:
                if m and (b, m) not in ff_out:
                    arrive(b, m)
                src = feats_ref.at[b] if m == 0 else slot(b, m)
                n = m + step
                f_out[b, n] = remote(src, slot(b, m), f_send.at[b, n], f_recv.at[b, n], same_core(step))
                f_out[b, n].start()

    loads[0].wait()
    loads[1].wait()
    f = feats[pl.ds(me * blocks, blocks)].reshape(rows_dev, width)
    gates = jax.nn.sigmoid(jnp.dot(f, pool[...], preferred_element_type=jnp.float32))
    pl.semaphore_wait(barrier, len(greet))
    gather_stage(0)
    pooled = tn_dot(gates.astype(jnp.bfloat16), f).reshape(groups, CORES, half, width)
    for h in range(CORES):
        part[h] = pooled[:, h]
        part_b[h] = pooled[:, h].astype(jnp.bfloat16)

    pair = remote(part_b.at[1 - core], pair_in, pair_sem.at[0], pair_sem.at[1], partner)
    pair.start()
    pair.wait_recv()
    part[core] = part[core] + pair_in[...].astype(jnp.float32)
    reduced[...] = part[core].astype(jnp.bfloat16)
    r_out = [None]
    for k in range(1, n_chips):
        to = xor(chip, k, bits)
        r_out.append(
            remote(reduced.at[to % groups], terms.at[k], r_send.at[k], r_recv.at[k], same_core(k))
        )
        r_out[k].start()
    for b in range(blocks):
        forward(b, 0)

    loads[2].wait()
    turned = jnp.transpose(start[...])
    state = jnp.where(core == 0, turned[:half], turned[half:])
    total = part[core, group]
    for k in range(1, n_chips):
        r_out[k].wait_recv()
        total = total + terms[k].astype(jnp.float32)
    sums[t_me] = (total * (rows_dev * n_dom) ** (-0.5)).astype(jnp.bfloat16)

    z_out = []
    for o in range(1, n_tm):
        z_out.append(
            remote(
                sums.at[t_me], sums.at[t_me], z_send.at[o], z_recv.at[t_me],
                {"tm": (t_me + o) % n_tm},
            )
        )
        z_out[-1].start()

    for i in range(1, bits):
        gather_stage(i)

    for i in range(3, 10):
        loads[i].wait()
    for j in range(slots):
        tile = vals[j]
        live = j < used_ref[0, 0]
        row = rows_ref[0, j] - me * blocks
        for b in range(blocks):
            mask[b * BLOCK:(b + 1) * BLOCK, j * BLOCK:(j + 1) * BLOCK] = jnp.where(
                live & (row == b), tile, jnp.zeros_like(tile)
            )
    for t in range(n_tm):
        @pl.when(t_me != t)
        def _(t=t):
            remote(sums.at[t], sums.at[t], z_send.at[0], z_recv.at[t], partner).wait_recv()

    every = sums[...].reshape(n_tm * half, width)
    inputs = [nt_dot(every, win[g]).reshape(n_tm, half, width) for g in range(3)]
    own_w = wfull.at[group, pl.ds(core * half, half)]
    for t in range(n_tm):
        state_b = state.astype(jnp.bfloat16)
        reset = jax.nn.sigmoid(inputs[1][t] + nt_dot(state_b, wst[1]))
        reset_state = (reset * state).astype(jnp.bfloat16)
        update = jax.nn.sigmoid(inputs[0][t] + nt_dot(state_b, wst[0]) - off[...])
        candidate = jnp.tanh(inputs[2][t] + nt_dot(reset_state, wst[2]))
        state = (1.0 - update) * state + update * candidate

        @pl.when(t_me == t)
        def _(state=state):
            own_w[...] = state.astype(jnp.bfloat16)

    w_out = [None]
    for k in range(1, groups):
        w_out.append(remote(own_w, own_w, w_send.at[k], w_recv.at[k], same_core(k)))
        w_out[k].start()
    wf_out = [remote(own_w, own_w, wf_send.at[0], wf_recv.at[0], partner)]
    wf_out[0].start()

    for key in list(f_out):
        if key not in ff_out:
            arrive(*key)
    for copy in ff_out.values():
        copy.wait_recv()
    sources = [feats[cols_ref[0, j]] for j in range(slots)]
    own = feats[pl.ds(me * blocks, blocks)].reshape(rows_dev, width).astype(jnp.float32)
    summed = jnp.dot(
        mask[...],
        jnp.concatenate(sources, axis=0),
        preferred_element_type=jnp.float32,
    )
    agg[...] = (own + summed).astype(jnp.bfloat16)

    for k in range(1, groups):
        w_out[k].wait_recv()
        ref = wfull.at[xor(group, k, bits), pl.ds(core * half, half)]
        wf_out.append(remote(ref, ref, wf_send.at[k], wf_recv.at[k], partner))
        wf_out[k].start()
    for k in range(groups):
        wf_out[k].wait_recv()
        g = xor(group, k, bits)
        w = wfull[g]
        lanes = pl.ds(pl.multiple_of(g * LANES, LANES), LANES)
        mixed = nt_dot(agg[...], w)
        hid_ref[:, lanes] = jnp.maximum(mixed * width ** (-0.5), 0.0).astype(jnp.bfloat16)
        wout_ref[:, lanes] = jnp.transpose(w.astype(jnp.float32))

    pair.wait_send()
    for copy in (
        r_out[1:] + list(f_out.values()) + list(ff_out.values()) + z_out + w_out[1:] + wf_out
    ):
        copy.wait_send()


def shards(
    n_dom,
    n_tm,
    features,
    tile_rows,
    tile_cols,
    tile_vals,
    tile_used,
    pool_weight,
    w_in,
    w_state,
    gate_offset,
    start_weight,
):
    _, rows_dev, width = features.shape
    slots = tile_rows.shape[1]
    blocks = rows_dev // BLOCK
    n_chips = n_dom // CORES
    groups = width // LANES
    hbm = pl.BlockSpec(memory_space=pltpu.HBM)
    vmem = pl.BlockSpec(memory_space=pltpu.VMEM)
    dma = pltpu.SemaphoreType.DMA
    bf16, f32 = jnp.bfloat16, jnp.float32
    half = LANES // CORES
    hidden, weights = pl.pallas_call(
        functools.partial(kernel, n_dom, n_tm),
        out_shape=(
            jax.ShapeDtypeStruct((rows_dev, width), bf16),
            jax.ShapeDtypeStruct((width, width), jnp.float32),
        ),
        in_specs=[hbm] * 10,
        out_specs=(vmem, vmem),
        scratch_shapes=[
            pltpu.VMEM((n_dom * blocks, BLOCK, width), bf16),
            pltpu.VMEM((slots, BLOCK, BLOCK), bf16),
            pltpu.VMEM((width, width), bf16),
            pltpu.VMEM((3, width, width), bf16),
            pltpu.VMEM((3, width, width), bf16),
            pltpu.VMEM((1, width), f32),
            pltpu.VMEM((width, LANES), f32),
            pltpu.VMEM((CORES, groups, half, width), f32),
            pltpu.VMEM((CORES, groups, half, width), bf16),
            pltpu.VMEM((groups, half, width), bf16),
            pltpu.VMEM((groups, half, width), bf16),
            pltpu.VMEM((n_chips, half, width), bf16),
            pltpu.VMEM((n_tm, half, width), bf16),
            pltpu.VMEM((groups, LANES, width), bf16),
            pltpu.VMEM((rows_dev, width), bf16),
            pltpu.VMEM((rows_dev, slots * BLOCK), bf16),
            pltpu.SMEM((1, slots), jnp.int32),
            pltpu.SMEM((1, slots), jnp.int32),
            pltpu.SMEM((1, 1), jnp.int32),
            dma((10,)),
            dma((2,)),
            dma((n_chips,)),
            dma((n_chips,)),
            dma((blocks, n_chips)),
            dma((blocks, n_chips)),
            dma((blocks, n_chips)),
            dma((blocks, n_chips)),
            dma((n_tm,)),
            dma((n_tm,)),
            dma((groups,)),
            dma((groups,)),
            dma((groups,)),
            dma((groups,)),
        ],
        compiler_params=pltpu.CompilerParams(
            collective_id=0, has_side_effects=True, vmem_limit_bytes=60 * 1024 * 1024
        ),
    )(
        features.reshape(blocks, BLOCK, width),
        tile_rows,
        tile_cols,
        tile_vals.reshape(slots, BLOCK, BLOCK),
        tile_used,
        pool_weight,
        w_in,
        w_state,
        gate_offset.reshape(1, width),
        start_weight,
    )
    return hidden[None], weights[None]


def solution(mesh):
    in_specs = (
        P("tm", "dom", None),
        P("tm", "dom"),
        P("tm", "dom"),
        P("tm", "dom", None, None),
        P("tm", "dom"),
        P(),
        P(),
        P(),
        P(),
        P(),
    )
    out_specs = (P("tm", "dom", None), P("tm", None, None))
    body = functools.partial(shards, mesh.shape["dom"], mesh.shape["tm"])
    return jax.shard_map(body, mesh=mesh, in_specs=in_specs, out_specs=out_specs, check_vma=False)
```

```python
import functools

import jax
import jax.numpy as jnp
from jax import lax
from jax.experimental import pallas as pl
from jax.experimental.pallas import tpu as pltpu
from jax.sharding import PartitionSpec as P

BLOCK = 128
LANES = 128
CORES = 2


def xor(q, k, bits):
    out = 0
    for b in range(bits):
        out = out + (((q // (1 << b)) + ((k >> b) & 1)) % 2) * (1 << b)
    return out


def nt_dot(a, b):
    return lax.dot_general(a, b, (((1,), (1,)), ((), ())), preferred_element_type=jnp.float32)


def tn_dot(a, b):
    return lax.dot_general(a, b, (((0,), (0,)), ((), ())), preferred_element_type=jnp.float32)


def kernel(
    n_dom,
    n_tm,
    feats_ref,
    rows_in,
    cols_in,
    vals_ref,
    used_in,
    pool_ref,
    win_ref,
    wst_ref,
    off_ref,
    start_ref,
    hid_ref,
    wout_ref,
    feats,
    vals,
    pool,
    win,
    wst,
    off,
    start,
    part,
    part_b,
    pair_in,
    reduced,
    terms,
    sums,
    wfull,
    agg,
    mask,
    rows_ref,
    cols_ref,
    used_ref,
    load_sem,
    pair_sem,
    r_send,
    r_recv,
    f_send,
    f_recv,
    ff_send,
    ff_recv,
    z_send,
    z_recv,
    w_send,
    w_recv,
    wf_send,
    wf_recv,
):
    n_chips = n_dom // CORES
    bits = n_chips.bit_length() - 1
    blocks, _, width = feats_ref.shape
    slots = vals_ref.shape[0]
    groups = wfull.shape[0]
    half = LANES // CORES
    rows_dev = blocks * BLOCK
    me = lax.axis_index("dom")
    t_me = lax.axis_index("tm")
    chip, core = me // CORES, me % CORES
    group = chip % groups
    partner = {"dom": chip * CORES + 1 - core}
    lane0 = pl.multiple_of(group * LANES, LANES)

    def same_core(k):
        return {"dom": xor(chip, k, bits) * CORES + core}

    def remote(src, dst, send, recv, to):
        return pltpu.make_async_remote_copy(
            src_ref=src, dst_ref=dst, send_sem=send, recv_sem=recv,
            device_id=to, device_id_type=pl.DeviceIdType.MESH,
        )

    def load(src, dst, i):
        copy = pltpu.make_async_copy(src, dst, load_sem.at[i])
        copy.start()
        return copy

    def piece(dev):
        return feats.at[pl.ds(dev * blocks, blocks)]

    loads = [
        load(feats_ref, piece(me), 0),
        load(pool_ref, pool, 1),
        load(start_ref.at[:, pl.ds(lane0, LANES)], start, 2),
        load(win_ref, win, 3),
        load(wst_ref, wst, 4),
        load(off_ref, off, 5),
        load(vals_ref, vals, 6),
        load(rows_in, rows_ref, 7),
        load(cols_in, cols_ref, 8),
        load(used_in, used_ref, 9),
    ]

    barrier = pltpu.get_barrier_semaphore()
    greet = [partner] + [same_core(k) for k in range(1, n_chips)]
    greet += [{"tm": (t_me + o) % n_tm} for o in range(1, n_tm)]
    for to in greet:
        pl.semaphore_signal(barrier, inc=1, device_id=to, device_id_type=pl.DeviceIdType.MESH)

    orders = [list(range(bits)) if b % 2 == 0 else list(range(bits))[::-1] for b in range(blocks)]
    f_out, ff_out = {}, {}

    def forward(b, m):
        src = feats_ref.at[b] if m == 0 else slot(b, m)
        ff_out[b, m] = remote(src, slot(b, m), ff_send.at[b, m], ff_recv.at[b, m], partner)
        ff_out[b, m].start()

    def slot(b, m):
        return feats.at[(xor(chip, m, bits) * CORES + core) * blocks + b]

    def arrive(b, m):
        f_out[b, m].wait_recv()
        forward(b, m)

    def gather_stage(i):
        for b in range(blocks):
            held = [0]
            for d in orders[b][:i]:
                held = held + [m + (1 << d) for m in held]
            step = 1 << orders[b][i]
            for m in held:
                if m and (b, m) not in ff_out:
                    arrive(b, m)
                src = feats_ref.at[b] if m == 0 else slot(b, m)
                n = m + step
                f_out[b, n] = remote(src, slot(b, m), f_send.at[b, n], f_recv.at[b, n], same_core(step))
                f_out[b, n].start()

    loads[0].wait()
    loads[1].wait()
    f = feats[pl.ds(me * blocks, blocks)].reshape(rows_dev, width)
    gates = jax.nn.sigmoid(jnp.dot(f, pool[...], preferred_element_type=jnp.float32))
    pl.semaphore_wait(barrier, len(greet))
    gather_stage(0)
    pooled = tn_dot(gates.astype(jnp.bfloat16), f).reshape(groups, CORES, half, width)
    for h in range(CORES):
        part[h] = pooled[:, h]
        part_b[h] = pooled[:, h].astype(jnp.bfloat16)

    pair = remote(part_b.at[1 - core], pair_in, pair_sem.at[0], pair_sem.at[1], partner)
    pair.start()
    pair.wait_recv()
    part[core] = part[core] + pair_in[...].astype(jnp.float32)
    reduced[...] = part[core].astype(jnp.bfloat16)
    r_out = [None]
    for k in range(1, n_chips):
        to = xor(chip, k, bits)
        r_out.append(
            remote(reduced.at[to % groups], terms.at[k], r_send.at[k], r_recv.at[k], same_core(k))
        )
        r_out[k].start()
    for b in range(blocks):
        forward(b, 0)

    loads[2].wait()
    turned = jnp.transpose(start[...])
    state = jnp.where(core == 0, turned[:half], turned[half:])
    total = part[core, group]
    for k in range(1, n_chips):
        r_out[k].wait_recv()
        total = total + terms[k].astype(jnp.float32)
    sums[t_me] = (total * (rows_dev * n_dom) ** (-0.5)).astype(jnp.bfloat16)

    z_out = []
    for o in range(1, n_tm):
        z_out.append(
            remote(
                sums.at[t_me], sums.at[t_me], z_send.at[o], z_recv.at[t_me],
                {"tm": (t_me + o) % n_tm},
            )
        )
        z_out[-1].start()

    for i in range(1, bits):
        gather_stage(i)

    for i in range(3, 10):
        loads[i].wait()
    for j in range(slots):
        tile = vals[j]
        live = j < used_ref[0, 0]
        row = rows_ref[0, j] - me * blocks
        for b in range(blocks):
            mask[b * BLOCK:(b + 1) * BLOCK, j * BLOCK:(j + 1) * BLOCK] = jnp.where(
                live & (row == b), tile, jnp.zeros_like(tile)
            )
    for t in range(n_tm):
        @pl.when(t_me != t)
        def _(t=t):
            remote(sums.at[t], sums.at[t], z_send.at[0], z_recv.at[t], partner).wait_recv()

    every = sums[...].reshape(n_tm * half, width)
    inputs = [nt_dot(every, win[g]).reshape(n_tm, half, width) for g in range(3)]
    own_w = wfull.at[group, pl.ds(core * half, half)]
    for t in range(n_tm):
        state_b = state.astype(jnp.bfloat16)
        reset = jax.nn.sigmoid(inputs[1][t] + nt_dot(state_b, wst[1]))
        reset_state = (reset * state).astype(jnp.bfloat16)
        update = jax.nn.sigmoid(inputs[0][t] + nt_dot(state_b, wst[0]) - off[...])
        candidate = jnp.tanh(inputs[2][t] + nt_dot(reset_state, wst[2]))
        state = (1.0 - update) * state + update * candidate

        @pl.when(t_me == t)
        def _(state=state):
            own_w[...] = state.astype(jnp.bfloat16)

    w_out = [None]
    for k in range(1, groups):
        w_out.append(remote(own_w, own_w, w_send.at[k], w_recv.at[k], same_core(k)))
        w_out[k].start()
    wf_out = [remote(own_w, own_w, wf_send.at[0], wf_recv.at[0], partner)]
    wf_out[0].start()

    for key in list(f_out):
        if key not in ff_out:
            arrive(*key)
    for copy in ff_out.values():
        copy.wait_recv()
    sources = [feats[cols_ref[0, j]] for j in range(slots)]
    own = feats[pl.ds(me * blocks, blocks)].reshape(rows_dev, width).astype(jnp.float32)
    summed = jnp.dot(
        mask[...],
        jnp.concatenate(sources, axis=0),
        preferred_element_type=jnp.float32,
    )
    agg[...] = (own + summed).astype(jnp.bfloat16)

    for k in range(1, groups):
        w_out[k].wait_recv()
        ref = wfull.at[xor(group, k, bits), pl.ds(core * half, half)]
        wf_out.append(remote(ref, ref, wf_send.at[k], wf_recv.at[k], partner))
        wf_out[k].start()
    for k in range(groups):
        wf_out[k].wait_recv()
        g = xor(group, k, bits)
        w = wfull[g]
        lanes = pl.ds(pl.multiple_of(g * LANES, LANES), LANES)
        mixed = nt_dot(agg[...], w)
        hid_ref[:, lanes] = jnp.maximum(mixed * width ** (-0.5), 0.0).astype(jnp.bfloat16)
        wout_ref[:, lanes] = jnp.transpose(w.astype(jnp.float32))

    pair.wait_send()
    for copy in (
        r_out[1:] + list(f_out.values()) + list(ff_out.values()) + z_out + w_out[1:] + wf_out
    ):
        copy.wait_send()


def in_hbm(x):
    return pltpu.with_memory_space_constraint(x, pltpu.HBM)


def shards(
    n_dom,
    n_tm,
    features,
    tile_rows,
    tile_cols,
    tile_vals,
    tile_used,
    pool_weight,
    w_in,
    w_state,
    gate_offset,
    start_weight,
):
    _, rows_dev, width = features.shape
    slots = tile_rows.shape[1]
    blocks = rows_dev // BLOCK
    n_chips = n_dom // CORES
    groups = width // LANES
    hbm = pl.BlockSpec(memory_space=pltpu.HBM)
    vmem = pl.BlockSpec(memory_space=pltpu.VMEM)
    dma = pltpu.SemaphoreType.DMA
    bf16, f32 = jnp.bfloat16, jnp.float32
    half = LANES // CORES
    hidden, weights = pl.pallas_call(
        functools.partial(kernel, n_dom, n_tm),
        out_shape=(
            pltpu.VMEM((rows_dev, width), bf16),
            pltpu.VMEM((width, width), f32),
        ),
        in_specs=[hbm] * 10,
        out_specs=(vmem, vmem),
        scratch_shapes=[
            pltpu.VMEM((n_dom * blocks, BLOCK, width), bf16),
            pltpu.VMEM((slots, BLOCK, BLOCK), bf16),
            pltpu.VMEM((width, width), bf16),
            pltpu.VMEM((3, width, width), bf16),
            pltpu.VMEM((3, width, width), bf16),
            pltpu.VMEM((1, width), f32),
            pltpu.VMEM((width, LANES), f32),
            pltpu.VMEM((CORES, groups, half, width), f32),
            pltpu.VMEM((CORES, groups, half, width), bf16),
            pltpu.VMEM((groups, half, width), bf16),
            pltpu.VMEM((groups, half, width), bf16),
            pltpu.VMEM((n_chips, half, width), bf16),
            pltpu.VMEM((n_tm, half, width), bf16),
            pltpu.VMEM((groups, LANES, width), bf16),
            pltpu.VMEM((rows_dev, width), bf16),
            pltpu.VMEM((rows_dev, slots * BLOCK), bf16),
            pltpu.SMEM((1, slots), jnp.int32),
            pltpu.SMEM((1, slots), jnp.int32),
            pltpu.SMEM((1, 1), jnp.int32),
            dma((10,)),
            dma((2,)),
            dma((n_chips,)),
            dma((n_chips,)),
            dma((blocks, n_chips)),
            dma((blocks, n_chips)),
            dma((blocks, n_chips)),
            dma((blocks, n_chips)),
            dma((n_tm,)),
            dma((n_tm,)),
            dma((groups,)),
            dma((groups,)),
            dma((groups,)),
            dma((groups,)),
        ],
        compiler_params=pltpu.CompilerParams(
            collective_id=0, has_side_effects=True, vmem_limit_bytes=48 * 1024 * 1024
        ),
    )(
        in_hbm(features.reshape(blocks, BLOCK, width)),
        in_hbm(tile_rows),
        in_hbm(tile_cols),
        in_hbm(tile_vals.reshape(slots, BLOCK, BLOCK)),
        tile_used,
        in_hbm(pool_weight),
        in_hbm(w_in),
        in_hbm(w_state),
        in_hbm(gate_offset.reshape(1, width)),
        in_hbm(start_weight),
    )
    return hidden[None], weights[None]


def solution(mesh):
    in_specs = (
        P("tm", "dom", None),
        P("tm", "dom"),
        P("tm", "dom"),
        P("tm", "dom", None, None),
        P("tm", "dom"),
        P(),
        P(),
        P(),
        P(),
        P(),
    )
    out_specs = (P("tm", "dom", None), P("tm", None, None))
    body = functools.partial(shards, mesh.shape["dom"], mesh.shape["tm"])
    return jax.shard_map(body, mesh=mesh, in_specs=in_specs, out_specs=out_specs, check_vma=False)
```
